32 devices in a mesh: seq: 8 (over z, y), ch: 4 (over x, core).
Axes of the slice: x: 2, y: 2, z: 4, core: 2. Of those that a mesh axis runs over, the one named last changes fastest.
Arguments:
- inputs: bfloat16 [256, 4096], P('ch', 'seq'), may hold values from -6 to 6
- cotangent: bfloat16 [256, 4096], P('ch', 'seq'), may hold values from -8 to 8
- w_in: bfloat16 [3, 256, 256], P(None, None, 'ch'), may hold values from -0.375 to 0.375
- short_taps: float32 [3, 3, 256], P(None, None, 'ch'), may hold values from -3 to 3
- filter_one: float32 [256, 4096], P('ch', 'seq'), may hold values from -1 to 1
- filter_two: float32 [256, 4096], P('ch', 'seq'), may hold values from -1 to 1
- w_out: bfloat16 [256, 256], P('ch'), may hold values from -0.375 to 0.375
Outputs:
- inputs_grad: bfloat16 [256, 4096], P('ch', 'seq')
- w_in_grad: float32 [3, 256, 256], P(None, 'seq', 'ch')
- taps_grad: float32 [3, 3, 256], P(None, None, 'ch')
- filter_one_grad: float32 [256, 4096], P('ch', 'seq')
- filter_two_grad: float32 [256, 4096], P('ch', 'seq')
- w_out_grad: float32 [256, 256], P('ch', 'seq')
The draws below stay inside these ranges and needn't reach their ends.
All inputs are finite; a program needn't handle non-finite values.
Results may differ from the reference program's by a relative error of at most 0.0051.
Values may be sent and summed in bfloat16 or wider, within the bound.
A program may use at most 64 MiB of HBM per device.

```python
import math
import jax
import jax.numpy as jnp
from jax import lax

D = 256
TOKENS = 4096


def make_filter(key):
    key_noise, key_mix, key_fast, key_slow = jax.random.split(key, 4)
    slow_share = 0.5
    noise = jax.random.truncated_normal(key_noise, -3.0, 3.0, (D, TOKENS), jnp.float32)
    choose_slow = jax.random.uniform(key_mix, (D,), jnp.float32) < slow_share
    fast_rate = jnp.exp(jax.random.uniform(key_fast, (D,), jnp.float32, math.log(1.0 / 50.0), math.log(1.0 / 30.0)))
    slow_rate = jnp.exp(jax.random.uniform(key_slow, (D,), jnp.float32, math.log(0.1), math.log(2.0))) / TOKENS
    rate = jnp.where(choose_slow, slow_rate, fast_rate)
    factor = jnp.sqrt(2.0 * rate / (1.0 - jnp.exp(-2.0 * rate * TOKENS)))
    position = jnp.arange(TOKENS, dtype=jnp.float32)[None, :]
    return (noise * jnp.exp(-rate[:, None] * position) * factor[:, None]).astype(jnp.float32)


def draw_filter_one(key, part):
    return make_filter(jax.random.fold_in(key, 11))


def draw_filter_two(key, part):
    return make_filter(jax.random.fold_in(key, 23))


def draw_cotangent(key, part):
    position = jnp.arange(TOKENS, dtype=jnp.float32)[None, :] / (TOKENS - 1)
    values = jax.random.truncated_normal(key, -2.5, 2.5, (D, TOKENS), jnp.float32) * (1.0 + 2.0 * position)
    return values.astype(jnp.bfloat16)


def with_spikes(drawn, key, source, target, shards_of, factor):
    def block_of(dim):
        return (jnp.arange(drawn.shape[dim]) // (drawn.shape[dim] // shards_of)).reshape((-1,) + (1,) * (drawn.ndim - 1 - dim))

    near = jax.random.permutation(key, shards_of)[block_of(target)]
    far = (block_of(target) + shards_of // 2) % shards_of
    return jnp.where((block_of(source) == near) | (block_of(source) == far), factor * drawn, drawn)


def block_levels(rng, shape, cuts, least, high):
    loudness = 1.0
    for axis_at, blocks in cuts:
        heights = jax.random.uniform(jax.random.fold_in(jax.random.fold_in(rng, 6), axis_at), (blocks,), jnp.float32, least / len(cuts), high / len(cuts))
        loudness = loudness * jnp.repeat(jnp.exp(heights), shape[axis_at] // blocks).reshape((-1,) + (1,) * (len(shape) - 1 - axis_at))
    return loudness


def gaussian(stream_key, shape, deviation, most, pieces=(), held_as=jnp.bfloat16):
    factor_of = block_levels(stream_key, shape, pieces, -0.22, 0.18) if pieces else 1.0
    array = jax.random.normal(stream_key, shape, jnp.float32) * deviation * factor_of
    return jnp.minimum(jnp.maximum(array, -most), most).astype(held_as)


def heavy_noise(own_key, dims, spread, most, pieces, heavy, held_as=jnp.bfloat16):
    entries = spread * jax.random.normal(own_key, dims, jnp.float32)
    if pieces:
        entries = entries * block_levels(own_key, dims, pieces, -0.22, 0.18)
    return jnp.clip(with_spikes(entries, jax.random.fold_in(own_key, 3), *heavy), -most, most).astype(held_as)


def setup_inputs(seed: int = 0) -> dict:
    streams_of = jax.random.split(jax.random.key(seed), 8)
    return {
        "inputs": heavy_noise(streams_of[0], (D, TOKENS), 1.0, 6.0, ((0, 4), (1, 8)), (1, 0, 8, 2.0)),
        "cotangent": draw_cotangent(jax.random.fold_in(streams_of[7], 71), 0),
        "w_in": gaussian(streams_of[2], (3, D, D), D ** -0.5, 0.375, ((2, 4),)),
        "short_taps": gaussian(streams_of[3], (3, 3, D), 0.5, 3.0, ((2, 4),), jnp.float32),
        "filter_one": draw_filter_one(jax.random.fold_in(streams_of[7], 71), 0),
        "filter_two": draw_filter_two(jax.random.fold_in(streams_of[7], 71), 0),
        "w_out": gaussian(streams_of[6], (D, D), D ** -0.5, 0.375, ((0, 4),)),
    }


def long_corr(kernel_spec, grad_spec, length):
    return jnp.fft.irfft(jnp.conj(kernel_spec) * grad_spec, n=2 * length, axis=0)[:length]

def reference(inputs, cotangent, w_in, short_taps, filter_one, filter_two, w_out):
    inputs = inputs.T
    cotangent = cotangent.T
    filter_one = filter_one.T
    filter_two = filter_two.T
    length = inputs.shape[0]
    width = inputs.shape[1]
    scale = 1.0 / jnp.sqrt(jnp.float32(length))
    w_joined = w_in.transpose(1, 0, 2).reshape(width, 3 * width)
    projected = jnp.dot(inputs, w_joined, preferred_element_type=jnp.float32)
    taps = short_taps.transpose(1, 0, 2).reshape(3, 3 * width)
    padded = jnp.concatenate([jnp.zeros((2, 3 * width), projected.dtype), projected], axis=0)
    filtered = taps[0] * projected + taps[1] * padded[1:length + 1] + taps[2] * padded[:length]
    gate_one = filtered[:, :width]
    gate_two = filtered[:, width:2 * width]
    value = filtered[:, 2 * width:]
    size_fft = 2 * length
    spec_value = jnp.fft.rfft(value, n=size_fft, axis=0)
    spec_one = jnp.fft.rfft(filter_one, n=size_fft, axis=0)
    spec_two = jnp.fft.rfft(filter_two, n=size_fft, axis=0)
    first = jnp.fft.irfft(spec_value * spec_one, n=size_fft, axis=0)[:length]
    inner = gate_one * first
    spec_inner = jnp.fft.rfft(inner, n=size_fft, axis=0)
    second = jnp.fft.irfft(spec_inner * spec_two, n=size_fft, axis=0)[:length]
    gated = (gate_two * second).astype(jnp.bfloat16)
    w_out_grad = jnp.dot(gated.T, cotangent, preferred_element_type=jnp.float32) * scale
    gated_grad = jnp.dot(cotangent, w_out.T, preferred_element_type=jnp.float32)
    gate_two_grad = gated_grad * second
    second_grad = gated_grad * gate_two
    spec_second = jnp.fft.rfft(second_grad, n=size_fft, axis=0)
    inner_grad = long_corr(spec_two, spec_second, length)
    filter_two_grad = long_corr(spec_inner, spec_second, length) * scale
    gate_one_grad = inner_grad * first
    first_grad = inner_grad * gate_one
    spec_first = jnp.fft.rfft(first_grad, n=size_fft, axis=0)
    value_grad = long_corr(spec_one, spec_first, length)
    filter_one_grad = long_corr(spec_value, spec_first, length) * scale
    filtered_grad = jnp.concatenate([gate_one_grad, gate_two_grad, value_grad], axis=1)
    tap_terms = jnp.stack([lax.optimization_barrier(jnp.sum(filtered_grad * projected, axis=0)), lax.optimization_barrier(jnp.sum(filtered_grad * padded[1:length + 1], axis=0)), lax.optimization_barrier(jnp.sum(filtered_grad * padded[:length], axis=0))]) * scale
    taps_grad = tap_terms.reshape(3, 3, width).transpose(1, 0, 2)
    after = jnp.concatenate([filtered_grad, jnp.zeros((2, 3 * width), filtered_grad.dtype)], axis=0)
    projected_grad = (taps[0] * filtered_grad + taps[1] * after[1:length + 1] + taps[2] * after[2:length + 2]).astype(jnp.bfloat16)
    w_in_grad = (jnp.dot(inputs.T, projected_grad, preferred_element_type=jnp.float32) * scale).reshape(width, 3, width).transpose(1, 0, 2)
    inputs_grad = jnp.dot(w_joined, projected_grad.T, preferred_element_type=jnp.float32).astype(jnp.bfloat16)
    return (inputs_grad, w_in_grad, taps_grad, filter_one_grad.T, filter_two_grad.T, w_out_grad)
```

```python
import functools
import math

import jax
import jax.numpy as jnp
import ml_dtypes
import numpy as np
from jax import lax
from jax.experimental import pallas as pl
from jax.experimental.pallas import tpu as pltpu
from jax.sharding import PartitionSpec as P

LANES = 128
MESH = pl.DeviceIdType.MESH
BF16 = jnp.bfloat16
F32 = jnp.float32


def halves(table):
    high = table.astype(np.float32).astype(ml_dtypes.bfloat16)
    low = (table - high.astype(np.float64)).astype(np.float32).astype(ml_dtypes.bfloat16)
    return [high, low]


def dft_tables(tokens, chans):
    blocks = tokens // LANES
    size = 2 * tokens
    eye = np.eye(chans)
    place = np.arange(blocks, dtype=np.float64)
    half = np.arange(blocks, dtype=np.float64) + 0.5
    coarse = 2.0 * np.pi / (2 * blocks) * np.outer(half, place)
    cos_one, sin_one = np.cos(coarse), np.sin(coarse)
    forward_one = np.concatenate([np.kron(cos_one, eye), -np.kron(sin_one, eye)], axis=0)
    inverse_one = 2.0 / size * np.concatenate(
        [np.kron(cos_one.T, eye), -np.kron(sin_one.T, eye)], axis=1
    )
    lane = np.arange(LANES)
    fine = 2.0 * np.pi / LANES * (np.outer(lane, lane) % LANES)
    cos_two, sin_two = np.cos(fine), np.sin(fine)
    forward_two = np.block([[cos_two, -sin_two], [sin_two, cos_two]])
    inverse_two = np.block([[cos_two, sin_two], [-sin_two, cos_two]])
    twist = np.repeat(2.0 * np.pi / size * np.outer(half, lane), chans, axis=0)
    tables = halves(forward_one) + halves(inverse_one) + halves(forward_two) + halves(inverse_two)
    return tables + [np.cos(twist).astype(np.float32), np.sin(twist).astype(np.float32)]


def split(value):
    high = value.astype(BF16)
    return high, (value - high.astype(F32)).astype(BF16)


def dot(left, right):
    return jnp.dot(left, right, preferred_element_type=F32)


def dot_rows(left, right):
    return lax.dot_general(left, right, (((1,), (1,)), ((), ())), preferred_element_type=F32)


def kernel(
    seqs,
    groups,
    x_ref,
    g_ref,
    f1_ref,
    f2_ref,
    wt_ref,
    wj_ref,
    wo_ref,
    taps_ref,
    mf_hi,
    mf_lo,
    mi_hi,
    mi_lo,
    df_hi,
    df_lo,
    di_hi,
    di_lo,
    tc_ref,
    ts_ref,
    dx_ref,
    dw_ref,
    dt_ref,
    df1_ref,
    df2_ref,
    xg,
    filt_out,
    filt_in,
    sig_out,
    sig_in,
    gated_out,
    gated_in,
    fg_out,
    fg_in,
    pg_out,
    pg_in,
    grads,
    w_out_buf,
    w_in_buf,
    dx_out,
    dx_in,
    sems_x,
    sems_seq,
    sems_dx,
):
    chans, span = x_ref.shape
    own = chans // seqs
    parts = span // LANES
    piece = parts * own
    rows = piece * seqs
    width = chans * groups
    scale = 1.0 / math.sqrt(span * seqs)
    me = lax.axis_index("seq")
    mine = lax.axis_index("ch")

    barrier = pltpu.get_barrier_semaphore()
    for k in range(1, seqs):
        pl.semaphore_signal(
            barrier, inc=1, device_id=(lax.rem(me + k, seqs), mine), device_id_type=MESH
        )
    for k in range(1, groups):
        pl.semaphore_signal(
            barrier, inc=1, device_id=(me, lax.rem(mine + k, groups)), device_id_type=MESH
        )

    def fold(value, first, target, index):
        for q in range(parts):
            target[index + (pl.ds(q * own, own), slice(None))] = value[
                first : first + own, q * LANES : (q + 1) * LANES
            ]

    for j in range(seqs):
        fold(f1_ref[pl.ds(j * own, own), :], 0, filt_out, (j, 0))
        fold(f2_ref[pl.ds(j * own, own), :], 0, filt_out, (j, 1))

    pl.semaphore_wait(barrier, seqs - 1 + groups - 1)

    def remote(source, target, send_sem, recv_sem, device):
        copy = pltpu.make_async_remote_copy(
            src_ref=source,
            dst_ref=target,
            send_sem=send_sem,
            recv_sem=recv_sem,
            device_id=device,
            device_id_type=MESH,
        )
        copy.start()
        return copy

    x_copies = []
    for k in range(1, groups):
        peer = (me, lax.rem(mine + k, groups))
        for a, ref in enumerate((x_ref, g_ref)):
            x_copies.append(
                remote(ref, xg.at[a, mine], sems_x.at[0, a, k], sems_x.at[1, a, k], peer)
            )

    def exchange(out, into, kind):
        copies = []
        for k in range(1, seqs):
            to = lax.rem(me + k, seqs)
            copies.append(
                remote(
                    out.at[to], into.at[me], sems_seq.at[0, kind, k], sems_seq.at[1, kind, k], (to, mine)
                )
            )
        into[me] = out[me]
        return copies

    def finish(copies):
        for copy in copies:
            copy.wait()

    filt_copies = exchange(filt_out, filt_in, 0)
    xg[0, mine] = x_ref[...]
    xg[1, mine] = g_ref[...]
    finish(x_copies)
    x_all = xg[0].reshape(width, span)
    g_all = xg[1].reshape(width, span)
    projected = dot(wt_ref[...], x_all)
    gated_grad_here = dot(wo_ref[...], g_all)
    for j in range(seqs):
        for i in range(3):
            fold(projected, i * chans + j * own, sig_out, (j, i))
        fold(gated_grad_here, j * own, sig_out, (j, 3))
    sig_copies = exchange(sig_out, sig_in, 1)

    cos_twist = tc_ref[...]
    sin_twist = ts_ref[...]

    def left(table_hi, table_lo, value):
        high, low = split(value)
        return dot(table_hi[...], high) + dot(table_hi[...], low) + dot(table_lo[...], high)

    def right(value, table_hi, table_lo):
        high, low = split(value)
        return dot(high, table_hi[...]) + dot(low, table_hi[...]) + dot(high, table_lo[...])

    def forward(signals):
        joined = signals[0] if len(signals) == 1 else jnp.concatenate(signals, axis=1)
        coarse = left(mf_hi, mf_lo, joined)
        out = []
        for s in range(len(signals)):
            real = coarse[:rows, s * LANES : (s + 1) * LANES]
            imag = coarse[rows:, s * LANES : (s + 1) * LANES]
            turned = jnp.concatenate(
                [
                    real * cos_twist + imag * sin_twist,
                    imag * cos_twist - real * sin_twist,
                ],
                axis=1,
            )
            spectrum = right(turned, df_hi, df_lo)
            out.append((spectrum[:, :LANES], spectrum[:, LANES:]))
        return out

    def inverse(spectra):
        turned = []
        for real, imag in spectra:
            fine = right(jnp.concatenate([real, imag], axis=1), di_hi, di_lo)
            real, imag = fine[:, :LANES], fine[:, LANES:]
            turned.append(
                jnp.concatenate(
                    [
                        real * cos_twist - imag * sin_twist,
                        real * sin_twist + imag * cos_twist,
                    ],
                    axis=0,
                )
            )
        joined = turned[0] if len(turned) == 1 else jnp.concatenate(turned, axis=1)
        result = left(mi_hi, mi_lo, joined)
        return [result[:, s * LANES : (s + 1) * LANES] for s in range(len(spectra))]

    def times(a, b):
        return (a[0] * b[0] - a[1] * b[1], a[0] * b[1] + a[1] * b[0])

    def conj_times(a, b):
        return (a[0] * b[0] + a[1] * b[1], a[0] * b[1] - a[1] * b[0])

    finish(filt_copies)
    spec_one, spec_two = forward(
        [filt_in[:, 0].reshape(rows, LANES), filt_in[:, 1].reshape(rows, LANES)]
    )

    row = lax.broadcasted_iota(jnp.int32, (rows, LANES), 0)
    lane = lax.broadcasted_iota(jnp.int32, (rows, LANES), 1)

    def delayed(value, k):
        rolled = pltpu.roll(value, k, 1)
        before = jnp.where(row < own, 0.0, pltpu.roll(rolled, own, 0))
        return jnp.where(lane < k, before, rolled)

    def advanced(value, k):
        rolled = pltpu.roll(value, LANES - k, 1)
        after = jnp.where(row >= rows - own, 0.0, pltpu.roll(rolled, rows - own, 0))
        return jnp.where(lane >= LANES - k, after, rolled)

    def tap(i, k):
        tile = taps_ref[3 * i + k]
        return jnp.broadcast_to(tile[None], (rows // 8, 8, LANES)).reshape(rows, LANES)

    finish(sig_copies)

    def projection(i):
        value = sig_in[:, i].reshape(rows, LANES)
        return value, delayed(value, 1), delayed(value, 2)

    def filtered(i):
        now, one, two = projection(i)
        return tap(i, 0) * now + tap(i, 1) * one + tap(i, 2) * two

    gate_one = filtered(0)
    gate_two = filtered(1)
    value = filtered(2)
    gated_grad = sig_in[:, 3].reshape(rows, LANES)

    second_grad = gated_grad * gate_two
    spec_value, spec_second = forward([value, second_grad])
    (first, inner_grad) = inverse([times(spec_one, spec_value), conj_times(spec_two, spec_second)])
    inner = gate_one * first
    gate_one_grad = inner_grad * first
    first_grad = inner_grad * gate_one
    spec_inner, spec_first = forward([inner, first_grad])
    second, filter_two_grad = inverse(
        [times(spec_inner, spec_two), conj_times(spec_inner, spec_second)]
    )
    gated = gate_two * second
    gated_out[...] = gated.reshape(seqs, piece, LANES).astype(BF16)
    gated_copies = exchange(gated_out, gated_in, 2)
    value_grad, filter_one_grad = inverse(
        [conj_times(spec_one, spec_first), conj_times(spec_value, spec_first)]
    )
    gate_two_grad = gated_grad * second

    for i, grad in enumerate((gate_one_grad, gate_two_grad, value_grad)):
        back = tap(i, 0) * grad + tap(i, 1) * advanced(grad, 1) + tap(i, 2) * advanced(grad, 2)
        pg_out[:, i] = back.reshape(seqs, piece, LANES).astype(BF16)
    pg_copies = exchange(pg_out, pg_in, 3)
    fg_out[:, 0] = (filter_one_grad * scale).reshape(seqs, piece, LANES)
    fg_out[:, 1] = (filter_two_grad * scale).reshape(seqs, piece, LANES)
    fg_copies = exchange(fg_out, fg_in, 4)

    small_lane = lax.broadcasted_iota(jnp.int32, (8, LANES), 1)
    tap_terms = jnp.zeros((8, LANES), F32)
    for i, grad in enumerate((gate_one_grad, gate_two_grad, value_grad)):
        for k, shifted in enumerate(projection(i)):
            total = jnp.sum((grad * shifted).reshape(rows // 8, 8, LANES), axis=0)
            total = jnp.sum(total, axis=1, keepdims=True) * scale
            tap_terms = jnp.where(small_lane == 3 * i + k, total, tap_terms)
    dt_ref[me] = tap_terms
    tap_copies = []
    for k in range(1, seqs):
        to = lax.rem(me + k, seqs)
        tap_copies.append(
            remote(
                dt_ref.at[me], dt_ref.at[me], sems_seq.at[0, 5, k], sems_seq.at[1, 5, k], (to, mine)
            )
        )

    def unfold(value, first, source, target):
        for q in range(parts):
            target[pl.ds(first + source * own, own), q * LANES : (q + 1) * LANES] = value[
                q * own : (q + 1) * own, :
            ]

    finish(gated_copies)
    for j in range(seqs):
        unfold(gated_in[j].astype(F32), 3 * chans, j, grads)
    finish(pg_copies)
    for j in range(seqs):
        for i in range(3):
            unfold(pg_in[j, i].astype(F32), i * chans, j, grads)
    back_all = grads[...].astype(BF16)
    back_in = back_all[: 3 * chans]
    back_out = back_all[3 * chans :]

    dx_part = dot(wj_ref[...], back_in)
    dx_out[...] = dx_part.reshape(groups, chans, span).astype(BF16)
    dx_copies = []
    for k in range(1, groups):
        to = lax.rem(mine + k, groups)
        dx_copies.append(
            remote(dx_out.at[to], dx_in.at[mine], sems_dx.at[0, k], sems_dx.at[1, k], (me, to))
        )
    share = width // seqs
    w_out_buf[:, :, : 3 * chans] = (dot_rows(x_all, back_in) * scale).reshape(
        seqs, share, 3 * chans
    )
    w_out_buf[:, :, 3 * chans :] = (dot_rows(g_all, back_out) * scale).reshape(seqs, share, chans)
    w_copies = exchange(w_out_buf, w_in_buf, 6)
    dx_in[mine] = dx_out[mine]

    finish(fg_copies)
    for j in range(seqs):
        unfold(fg_in[j, 0], 0, j, df1_ref)
        unfold(fg_in[j, 1], 0, j, df2_ref)
    finish(tap_copies)
    finish(dx_copies)
    total = dx_in[0].astype(F32)
    for j in range(1, groups):
        total = total + dx_in[j].astype(F32)
    dx_ref[...] = total.astype(BF16)
    finish(w_copies)
    total = w_in_buf[0]
    for j in range(1, seqs):
        total = total + w_in_buf[j]
    dw_ref[...] = total


def local(inputs, cotangent, w_in, short_taps, filter_one, filter_two, w_out):
    chans, span = inputs.shape
    seqs = lax.axis_size("seq")
    groups = lax.axis_size("ch")
    width = chans * groups
    own = chans // seqs
    piece = span // LANES * own
    share = width // seqs
    me = lax.axis_index("seq")
    w_turned = w_in.transpose(0, 2, 1).reshape(3 * chans, width)
    w_joined = w_in.transpose(1, 0, 2).reshape(width, 3 * chans)
    taps = lax.dynamic_slice_in_dim(short_taps.reshape(9, chans), me * own, own, axis=1)
    taps = jnp.broadcast_to(jnp.tile(taps, (1, 8 // own))[:, :, None], (9, 8, LANES))
    tables = [jnp.asarray(table) for table in dft_tables(span * seqs, own)]
    vmem = pl.BlockSpec(memory_space=pltpu.VMEM)
    dx, dw, dt, df1, df2 = pl.pallas_call(
        functools.partial(kernel, seqs, groups),
        out_shape=(
            jax.ShapeDtypeStruct((chans, span), BF16),
            jax.ShapeDtypeStruct((share, 4 * chans), F32),
            jax.ShapeDtypeStruct((seqs, 8, LANES), F32),
            jax.ShapeDtypeStruct((chans, span), F32),
            jax.ShapeDtypeStruct((chans, span), F32),
        ),
        in_specs=[vmem] * (8 + len(tables)),
        out_specs=(vmem,) * 5,
        scratch_shapes=[
            pltpu.VMEM((2, groups, chans, span), BF16),
            pltpu.VMEM((seqs, 2, piece, LANES), F32),
            pltpu.VMEM((seqs, 2, piece, LANES), F32),
            pltpu.VMEM((seqs, 4, piece, LANES), F32),
            pltpu.VMEM((seqs, 4, piece, LANES), F32),
            pltpu.VMEM((seqs, piece, LANES), BF16),
            pltpu.VMEM((seqs, piece, LANES), BF16),
            pltpu.VMEM((seqs, 2, piece, LANES), F32),
            pltpu.VMEM((seqs, 2, piece, LANES), F32),
            pltpu.VMEM((seqs, 3, piece, LANES), BF16),
            pltpu.VMEM((seqs, 3, piece, LANES), BF16),
            pltpu.VMEM((4 * chans, span), F32),
            pltpu.VMEM((seqs, share, 4 * chans), F32),
            pltpu.VMEM((seqs, share, 4 * chans), F32),
            pltpu.VMEM((groups, chans, span), BF16),
            pltpu.VMEM((groups, chans, span), BF16),
            pltpu.SemaphoreType.DMA((2, 2, groups)),
            pltpu.SemaphoreType.DMA((2, 7, seqs)),
            pltpu.SemaphoreType.DMA((2, groups)),
        ],
        compiler_params=pltpu.CompilerParams(
            collective_id=0, has_side_effects=True, vmem_limit_bytes=40 * 1024 * 1024
        ),
    )(inputs, cotangent, filter_one, filter_two, w_turned, w_joined, w_out, taps, *tables)
    w_in_grad = dw[:, : 3 * chans].reshape(share, 3, chans).transpose(1, 0, 2)
    w_out_grad = dw[:, 3 * chans :].T
    taps_grad = dt[:, :, :9].reshape(seqs, 8 // own, own, 9).sum(axis=1)
    taps_grad = taps_grad.reshape(chans, 9).T.reshape(3, 3, chans)
    return (dx, w_in_grad, taps_grad, df1, df2, w_out_grad)


def solution(mesh):
    in_specs = (
        P("ch", "seq"),
        P("ch", "seq"),
        P(None, None, "ch"),
        P(None, None, "ch"),
        P("ch", "seq"),
        P("ch", "seq"),
        P("ch", None),
    )
    out_specs = (
        P("ch", "seq"),
        P(None, "seq", "ch"),
        P(None, None, "ch"),
        P("ch", "seq"),
        P("ch", "seq"),
        P("ch", "seq"),
    )
    return jax.shard_map(local, mesh=mesh, in_specs=in_specs, out_specs=out_specs, check_vma=False)
```

```python
import functools
import math

import jax
import jax.numpy as jnp
import ml_dtypes
import numpy as np
from jax import lax
from jax.experimental import pallas as pl
from jax.experimental.pallas import tpu as pltpu
from jax.sharding import PartitionSpec as P

LANES = 128
TABLES = 10
MESH = pl.DeviceIdType.MESH
BF16 = jnp.bfloat16
F32 = jnp.float32


def halves(table):
    high = table.astype(np.float32).astype(ml_dtypes.bfloat16)
    low = (table - high.astype(np.float64)).astype(np.float32).astype(ml_dtypes.bfloat16)
    return [high, low]


def dft_tables(tokens, chans):
    blocks = tokens // LANES
    size = 2 * tokens
    eye = np.eye(chans)
    place = np.arange(blocks, dtype=np.float64)
    half = np.arange(blocks, dtype=np.float64) + 0.5
    coarse = 2.0 * np.pi / (2 * blocks) * np.outer(half, place)
    cos_one, sin_one = np.cos(coarse), np.sin(coarse)
    forward_one = np.concatenate([np.kron(cos_one, eye), -np.kron(sin_one, eye)], axis=0)
    inverse_one = 2.0 / size * np.concatenate(
        [np.kron(cos_one.T, eye), -np.kron(sin_one.T, eye)], axis=1
    )
    lane = np.arange(LANES)
    fine = 2.0 * np.pi / LANES * (np.outer(lane, lane) % LANES)
    cos_two, sin_two = np.cos(fine), np.sin(fine)
    forward_two = np.block([[cos_two, -sin_two], [sin_two, cos_two]])
    inverse_two = np.block([[cos_two, sin_two], [-sin_two, cos_two]])
    twist = np.repeat(2.0 * np.pi / size * np.outer(half, lane), chans, axis=0)
    tables = halves(forward_one) + halves(inverse_one) + halves(forward_two) + halves(inverse_two)
    return tables + [np.cos(twist).astype(np.float32), np.sin(twist).astype(np.float32)]


def split(value):
    high = value.astype(BF16)
    return high, (value - high.astype(F32)).astype(BF16)


def dot(left, right):
    return jnp.dot(left, right, preferred_element_type=F32)


def dot_rows(left, right):
    return lax.dot_general(left, right, (((1,), (1,)), ((), ())), preferred_element_type=F32)


def spread(value, first, own, target):
    for q in range(target.shape[1] // LANES):
        target[first : first + own, q * LANES : (q + 1) * LANES] = value[q * own : (q + 1) * own]


def kernel(
    seqs,
    groups,
    x_ref,
    g_ref,
    f1_ref,
    f2_ref,
    w_ref,
    wo_ref,
    taps_ref,
    *rest,
):
    sources, rest = rest[:TABLES], rest[TABLES:]
    w_in_buf, dt_ref, fg_in, dx_in = rest[:4]
    tables, rest = rest[4 : 4 + TABLES], rest[4 + TABLES :]
    mf_hi, mf_lo, mi_hi, mi_lo, df_hi, df_lo, di_hi, di_lo, tc_ref, ts_ref = tables
    (
        filters,
        w_here,
        wo_here,
        xg,
        filt_out,
        filt_in,
        sig_fold,
        sig_out,
        sig_in,
        gated_out,
        gated_in,
        fg_out,
        pg_out,
        pg_in,
        grads,
        w_out_buf,
        dx_out,
        sems_x,
        sems_seq,
        sems_dx,
        sems_local,
    ) = rest
    chans, span = x_ref.shape
    own = chans // seqs
    parts = span // LANES
    piece = parts * own
    rows = piece * seqs
    width = chans * groups
    scale = 1.0 / math.sqrt(span * seqs)
    me = lax.axis_index("seq")
    mine = lax.axis_index("ch")

    barrier = pltpu.get_barrier_semaphore()
    for k in range(1, seqs):
        pl.semaphore_signal(
            barrier, inc=1, device_id=(lax.rem(me + k, seqs), mine), device_id_type=MESH
        )
    for k in range(1, groups):
        pl.semaphore_signal(
            barrier, inc=1, device_id=(me, lax.rem(mine + k, groups)), device_id_type=MESH
        )

    arrivals = [
        (f1_ref, filters.at[0]),
        (f2_ref, filters.at[1]),
        (w_ref, w_here),
        (wo_ref, wo_here),
        (x_ref, xg.at[0, mine]),
        (g_ref, xg.at[1, mine]),
    ] + list(zip(sources, tables))
    fetches = []
    for at, (source, target) in enumerate(arrivals):
        fetch = pltpu.make_async_copy(source, target, sems_local.at[at])
        fetch.start()
        fetches.append(fetch)

    def fold(value, first, target, index):
        for q in range(parts):
            target[index + (pl.ds(q * own, own), slice(None))] = value[
                first : first + own, q * LANES : (q + 1) * LANES
            ]

    pl.semaphore_wait(barrier, seqs - 1 + groups - 1)

    def remote(source, target, send_sem, recv_sem, device):
        copy = pltpu.make_async_remote_copy(
            src_ref=source,
            dst_ref=target,
            send_sem=send_sem,
            recv_sem=recv_sem,
            device_id=device,
            device_id_type=MESH,
        )
        copy.start()
        return copy

    x_copies = []
    for k in range(1, groups):
        peer = (me, lax.rem(mine + k, groups))
        for a, ref in enumerate((x_ref, g_ref)):
            x_copies.append(
                remote(ref, xg.at[a, mine], sems_x.at[0, a, k], sems_x.at[1, a, k], peer)
            )

    def exchange(out, into, kind):
        copies = []
        for k in range(1, seqs):
            to = lax.rem(me + k, seqs)
            copies.append(
                remote(
                    out.at[to], into.at[me], sems_seq.at[0, kind, k], sems_seq.at[1, kind, k], (to, mine)
                )
            )
        into[me] = out[me]
        return copies

    def finish(copies):
        for copy in copies:
            copy.wait()

    fetches[0].wait()
    fetches[1].wait()
    for j in range(seqs):
        for i in range(2):
            fold(filters[i, pl.ds(j * own, own), :], 0, filt_out, (j, i))
    filt_copies = exchange(filt_out, filt_in, 0)
    finish(fetches[2:])
    w_turned = w_here[...].reshape(3 * chans, width)
    finish(x_copies)
    x_all = xg[0].reshape(width, span)
    g_all = xg[1].reshape(width, span)
    projected = dot(w_turned, x_all)
    gated_grad_here = dot(wo_here[...], g_all)
    for j in range(seqs):
        for i in range(3):
            fold(projected, i * chans + j * own, sig_fold, (j, i))
        fold(gated_grad_here, j * own, sig_fold, (j, 3))
    sig_out[...] = sig_fold[...].astype(BF16)
    sig_copies = exchange(sig_out, sig_in, 1)

    cos_twist = tc_ref[...]
    sin_twist = ts_ref[...]

    def left(table_hi, table_lo, value):
        high, low = split(value)
        return dot(table_hi[...], high) + dot(table_hi[...], low) + dot(table_lo[...], high)

    def right(value, table_hi, table_lo):
        high, low = split(value)
        return dot(high, table_hi[...]) + dot(low, table_hi[...]) + dot(high, table_lo[...])

    def forward(signals):
        joined = signals[0] if len(signals) == 1 else jnp.concatenate(signals, axis=1)
        coarse = left(mf_hi, mf_lo, joined)
        out = []
        for s in range(len(signals)):
            real = coarse[:rows, s * LANES : (s + 1) * LANES]
            imag = coarse[rows:, s * LANES : (s + 1) * LANES]
            turned = jnp.concatenate(
                [
                    real * cos_twist + imag * sin_twist,
                    imag * cos_twist - real * sin_twist,
                ],
                axis=1,
            )
            spectrum = right(turned, df_hi, df_lo)
            out.append((spectrum[:, :LANES], spectrum[:, LANES:]))
        return out

    def inverse(spectra):
        turned = []
        for real, imag in spectra:
            fine = right(jnp.concatenate([real, imag], axis=1), di_hi, di_lo)
            real, imag = fine[:, :LANES], fine[:, LANES:]
            turned.append(
                jnp.concatenate(
                    [
                        real * cos_twist - imag * sin_twist,
                        real * sin_twist + imag * cos_twist,
                    ],
                    axis=0,
                )
            )
        joined = turned[0] if len(turned) == 1 else jnp.concatenate(turned, axis=1)
        result = left(mi_hi, mi_lo, joined)
        return [result[:, s * LANES : (s + 1) * LANES] for s in range(len(spectra))]

    def times(a, b):
        return (a[0] * b[0] - a[1] * b[1], a[0] * b[1] + a[1] * b[0])

    def conj_times(a, b):
        return (a[0] * b[0] + a[1] * b[1], a[0] * b[1] - a[1] * b[0])

    def gathered(block):
        return block.astype(F32).reshape(rows, LANES)

    finish(filt_copies)
    spec_one, spec_two = forward(
        [gathered(filt_in[:, 0]), gathered(filt_in[:, 1])]
    )

    row = lax.broadcasted_iota(jnp.int32, (rows, LANES), 0)
    lane = lax.broadcasted_iota(jnp.int32, (rows, LANES), 1)

    def delayed(value, k):
        rolled = pltpu.roll(value, k, 1)
        before = jnp.where(row < own, 0.0, pltpu.roll(rolled, own, 0))
        return jnp.where(lane < k, before, rolled)

    def advanced(value, k):
        rolled = pltpu.roll(value, LANES - k, 1)
        after = jnp.where(row >= rows - own, 0.0, pltpu.roll(rolled, rows - own, 0))
        return jnp.where(lane >= LANES - k, after, rolled)

    def tap(i, k):
        tile = taps_ref[3 * i + k]
        return jnp.broadcast_to(tile[None], (rows // 8, 8, LANES)).reshape(rows, LANES)

    finish(sig_copies)

    def projection(i):
        value = gathered(sig_in[:, i])
        return value, delayed(value, 1), delayed(value, 2)

    def filtered(i):
        now, one, two = projection(i)
        return tap(i, 0) * now + tap(i, 1) * one + tap(i, 2) * two

    gate_one = filtered(0)
    gate_two = filtered(1)
    value = filtered(2)
    gated_grad = gathered(sig_in[:, 3])

    second_grad = gated_grad * gate_two
    spec_value, spec_second = forward([value, second_grad])
    (first, inner_grad) = inverse([times(spec_one, spec_value), conj_times(spec_two, spec_second)])
    inner = gate_one * first
    gate_one_grad = inner_grad * first
    first_grad = inner_grad * gate_one
    spec_inner, spec_first = forward([inner, first_grad])
    second, filter_two_grad = inverse(
        [times(spec_inner, spec_two), conj_times(spec_inner, spec_second)]
    )
    gated = gate_two * second
    gated_out[...] = gated.reshape(seqs, piece, LANES).astype(BF16)
    gated_copies = exchange(gated_out, gated_in, 2)
    fg_out[1] = (filter_two_grad * scale).reshape(seqs, piece, LANES).astype(BF16)
    fg_copies = exchange(fg_out.at[1], fg_in.at[1], 4)
    value_grad, filter_one_grad = inverse(
        [conj_times(spec_one, spec_first), conj_times(spec_value, spec_first)]
    )
    gate_two_grad = gated_grad * second

    for i, grad in enumerate((gate_one_grad, gate_two_grad, value_grad)):
        back = tap(i, 0) * grad + tap(i, 1) * advanced(grad, 1) + tap(i, 2) * advanced(grad, 2)
        pg_out[:, i] = back.reshape(seqs, piece, LANES).astype(BF16)
    pg_copies = exchange(pg_out, pg_in, 3)
    fg_out[0] = (filter_one_grad * scale).reshape(seqs, piece, LANES).astype(BF16)
    fg_copies += exchange(fg_out.at[0], fg_in.at[0], 7)

    small_lane = lax.broadcasted_iota(jnp.int32, (8, LANES), 1)
    tap_terms = jnp.zeros((8, LANES), F32)
    for i, grad in enumerate((gate_one_grad, gate_two_grad, value_grad)):
        for k, shifted in enumerate(projection(i)):
            total = jnp.sum((grad * shifted).reshape(rows // 8, 8, LANES), axis=0)
            total = jnp.sum(total, axis=1, keepdims=True) * scale
            tap_terms = jnp.where(small_lane == 3 * i + k, total, tap_terms)
    dt_ref[me] = tap_terms
    tap_copies = []
    for k in range(1, seqs):
        to = lax.rem(me + k, seqs)
        tap_copies.append(
            remote(
                dt_ref.at[me], dt_ref.at[me], sems_seq.at[0, 5, k], sems_seq.at[1, 5, k], (to, mine)
            )
        )

    def unfold(value, first, source, target):
        spread(value, first + source * own, own, target)

    finish(gated_copies)
    for j in range(seqs):
        unfold(gated_in[j].astype(F32), 3 * chans, j, grads)
    finish(pg_copies)
    for j in range(seqs):
        for i in range(3):
            unfold(pg_in[j, i].astype(F32), i * chans, j, grads)
    back_all = grads[...].astype(BF16)
    back_in = back_all[: 3 * chans]
    back_out = back_all[3 * chans :]

    dx_part = lax.dot_general(
        w_turned, back_in, (((0,), (0,)), ((), ())), preferred_element_type=F32
    )
    dx_out[...] = dx_part.reshape(groups, chans, span)
    dx_copies = []
    for k in range(1, groups):
        to = lax.rem(mine + k, groups)
        dx_copies.append(
            remote(dx_out.at[to], dx_in.at[mine], sems_dx.at[0, k], sems_dx.at[1, k], (me, to))
        )
    share = width // seqs
    w_out_buf[:, :, : 3 * chans] = (dot_rows(x_all, back_in) * scale).reshape(
        seqs, share, 3 * chans
    ).astype(BF16)
    w_out_buf[:, :, 3 * chans :] = (dot_rows(g_all, back_out) * scale).reshape(seqs, share, chans).astype(BF16)
    w_copies = exchange(w_out_buf, w_in_buf, 6)
    dx_in[mine] = dx_out[mine]

    finish(fg_copies)
    finish(tap_copies)
    finish(dx_copies)
    finish(w_copies)


def closing(w_ref, dt_ref, fg_ref, dx_part_ref, dx_ref, dw_in_ref, taps_ref, df1_ref, df2_ref, dw_out_ref):
    seqs = w_ref.shape[0]
    chans = dx_ref.shape[0]
    own = chans // seqs
    for j in range(seqs):
        for ref, i in ((df1_ref, 0), (df2_ref, 1)):
            spread(fg_ref[i, j].astype(F32), j * own, own, ref)
    total = dx_part_ref[0].astype(F32)
    for j in range(1, dx_part_ref.shape[0]):
        total = total + dx_part_ref[j].astype(F32)
    dx_ref[...] = total.astype(BF16)
    total = w_ref[0].astype(F32)
    for j in range(1, seqs):
        total = total + w_ref[j].astype(F32)
    for i in range(3):
        dw_in_ref[i] = total[:, i * chans : (i + 1) * chans]
    dw_out_ref[...] = total[:, 3 * chans :]
    terms = []
    for j in range(seqs):
        term = dt_ref[j, 0:own]
        for r in range(own, 8, own):
            term = term + dt_ref[j, r : r + own]
        terms.append(term)
    turned = jnp.concatenate(terms, axis=0).T
    for i in range(3):
        taps_ref[i] = turned[3 * i : 3 * i + 3, :]


def local(inputs, cotangent, w_in, short_taps, filter_one, filter_two, w_out):
    chans, span = inputs.shape
    seqs = lax.axis_size("seq")
    groups = lax.axis_size("ch")
    width = chans * groups
    own = chans // seqs
    piece = span // LANES * own
    share = width // seqs
    me = lax.axis_index("seq")
    w_turned = w_in.transpose(0, 2, 1)
    taps = lax.dynamic_slice_in_dim(short_taps.reshape(9, chans), me * own, own, axis=1)
    taps = jnp.broadcast_to(jnp.tile(taps, (1, 8 // own))[:, :, None], (9, 8, LANES))
    tables = [jnp.asarray(table) for table in dft_tables(span * seqs, own)]
    vmem = pl.BlockSpec(memory_space=pltpu.VMEM)
    hbm = pl.BlockSpec(memory_space=pltpu.HBM)
    received = pl.pallas_call(
        functools.partial(kernel, seqs, groups),
        out_shape=(
            jax.ShapeDtypeStruct((seqs, share, 4 * chans), BF16),
            jax.ShapeDtypeStruct((seqs, 8, LANES), F32),
            jax.ShapeDtypeStruct((2, seqs, piece, LANES), BF16),
            jax.ShapeDtypeStruct((groups, chans, span), F32),
        ),
        in_specs=[hbm] * 6 + [vmem] + [hbm] * TABLES,
        out_specs=(vmem,) * 4,
        scratch_shapes=[pltpu.VMEM(table.shape, table.dtype) for table in tables]
        + [
            pltpu.VMEM((2, chans, span), F32),
            pltpu.VMEM(w_turned.shape, BF16),
            pltpu.VMEM(w_out.shape, BF16),
            pltpu.VMEM((2, groups, chans, span), BF16),
            pltpu.VMEM((seqs, 2, piece, LANES), F32),
            pltpu.VMEM((seqs, 2, piece, LANES), F32),
            pltpu.VMEM((seqs, 4, piece, LANES), F32),
            pltpu.VMEM((seqs, 4, piece, LANES), BF16),
            pltpu.VMEM((seqs, 4, piece, LANES), BF16),
            pltpu.VMEM((seqs, piece, LANES), BF16),
            pltpu.VMEM((seqs, piece, LANES), BF16),
            pltpu.VMEM((2, seqs, piece, LANES), BF16),
            pltpu.VMEM((seqs, 3, piece, LANES), BF16),
            pltpu.VMEM((seqs, 3, piece, LANES), BF16),
            pltpu.VMEM((4 * chans, span), F32),
            pltpu.VMEM((seqs, share, 4 * chans), BF16),
            pltpu.VMEM((groups, chans, span), F32),
            pltpu.SemaphoreType.DMA((2, 2, groups)),
            pltpu.SemaphoreType.DMA((2, 8, seqs)),
            pltpu.SemaphoreType.DMA((2, groups)),
            pltpu.SemaphoreType.DMA((6 + TABLES,)),
        ],
        compiler_params=pltpu.CompilerParams(
            collective_id=0, has_side_effects=True, vmem_limit_bytes=60 * 1024 * 1024
        ),
    )(inputs, cotangent, filter_one, filter_two, w_turned, w_out, taps, *tables)
    dx, w_in_grad, taps_grad, df1, df2, w_out_turned = (
        pl.pallas_call(
            closing,
            out_shape=(
                jax.ShapeDtypeStruct((chans, span), BF16),
                jax.ShapeDtypeStruct((3, share, chans), F32),
                jax.ShapeDtypeStruct((3, 3, chans), F32),
                jax.ShapeDtypeStruct((chans, span), F32),
                jax.ShapeDtypeStruct((chans, span), F32),
                jax.ShapeDtypeStruct((share, chans), F32),
            ),
            in_specs=[vmem] * 4,
            out_specs=(vmem,) * 6,
            compiler_params=pltpu.CompilerParams(vmem_limit_bytes=60 * 1024 * 1024),
        )(*received)
    )
    return (dx, w_in_grad, taps_grad, df1, df2, w_out_turned.T)


def solution(mesh):
    in_specs = (
        P("ch", "seq"),
        P("ch", "seq"),
        P(None, None, "ch"),
        P(None, None, "ch"),
        P("ch", "seq"),
        P("ch", "seq"),
        P("ch", None),
    )
    out_specs = (
        P("ch", "seq"),
        P(None, "seq", "ch"),
        P(None, None, "ch"),
        P("ch", "seq"),
        P("ch", "seq"),
        P("ch", "seq"),
    )
    return jax.shard_map(local, mesh=mesh, in_specs=in_specs, out_specs=out_specs, check_vma=False)
```

```python
import functools
import math

import jax
import jax.numpy as jnp
import ml_dtypes
import numpy as np
from jax import lax
from jax.experimental import pallas as pl
from jax.experimental.pallas import tpu as pltpu
from jax.sharding import PartitionSpec as P

LANES = 128
TABLES = 10
MESH = pl.DeviceIdType.MESH
BF16 = jnp.bfloat16
F32 = jnp.float32


def halves(table):
    high = table.astype(np.float32).astype(ml_dtypes.bfloat16)
    low = (table - high.astype(np.float64)).astype(np.float32).astype(ml_dtypes.bfloat16)
    return [high, low]


def dft_tables(tokens, chans):
    blocks = tokens // LANES
    size = 2 * tokens
    eye = np.eye(chans)
    place = np.arange(blocks, dtype=np.float64)
    half = np.arange(blocks, dtype=np.float64) + 0.5
    coarse = 2.0 * np.pi / (2 * blocks) * np.outer(half, place)
    cos_one, sin_one = np.cos(coarse), np.sin(coarse)
    forward_one = np.concatenate([np.kron(cos_one, eye), -np.kron(sin_one, eye)], axis=0)
    inverse_one = 2.0 / size * np.concatenate(
        [np.kron(cos_one.T, eye), -np.kron(sin_one.T, eye)], axis=1
    )
    lane = np.arange(LANES)
    fine = 2.0 * np.pi / LANES * (np.outer(lane, lane) % LANES)
    cos_two, sin_two = np.cos(fine), np.sin(fine)
    forward_two = np.block([[cos_two, -sin_two], [sin_two, cos_two]])
    inverse_two = np.block([[cos_two, sin_two], [-sin_two, cos_two]])
    twist = np.repeat(2.0 * np.pi / size * np.outer(half, lane), chans, axis=0)
    tables = halves(forward_one) + halves(inverse_one) + halves(forward_two) + halves(inverse_two)
    return tables + [np.cos(twist).astype(np.float32), np.sin(twist).astype(np.float32)]


def split(value):
    high = value.astype(BF16)
    return high, (value - high.astype(F32)).astype(BF16)


def dot(left, right):
    return jnp.dot(left, right, preferred_element_type=F32)


def dot_rows(left, right):
    return lax.dot_general(left, right, (((1,), (1,)), ((), ())), preferred_element_type=F32)


def spread(value, first, own, target):
    for q in range(target.shape[1] // LANES):
        target[first : first + own, q * LANES : (q + 1) * LANES] = value[q * own : (q + 1) * own]


def kernel(
    seqs,
    groups,
    x_ref,
    g_ref,
    f1_ref,
    f2_ref,
    w_ref,
    wo_ref,
    taps_ref,
    *rest,
):
    sources, rest = rest[:TABLES], rest[TABLES:]
    w_in_buf, dt_ref, fg_in, dx_in = rest[:4]
    tables, rest = rest[4 : 4 + TABLES], rest[4 + TABLES :]
    mf_hi, mf_lo, mi_hi, mi_lo, df_hi, df_lo, di_hi, di_lo, tc_ref, ts_ref = tables
    (
        filters,
        w_here,
        wo_here,
        xg,
        filt_out,
        filt_in,
        sig_fold,
        sig_out,
        sig_in,
        gg_out,
        gg_in,
        gated_out,
        gated_in,
        fg_out,
        pg_out,
        pg_in,
        grads,
        w_out_buf,
        dx_out,
        sems_x,
        sems_seq,
        sems_dx,
        sems_local,
    ) = rest
    chans, span = x_ref.shape
    own = chans // seqs
    parts = span // LANES
    piece = parts * own
    rows = piece * seqs
    width = chans * groups
    scale = 1.0 / math.sqrt(span * seqs)
    me = lax.axis_index("seq")
    mine = lax.axis_index("ch")

    barrier = pltpu.get_barrier_semaphore()
    for k in range(1, seqs):
        pl.semaphore_signal(
            barrier, inc=1, device_id=(lax.rem(me + k, seqs), mine), device_id_type=MESH
        )
    for k in range(1, groups):
        pl.semaphore_signal(
            barrier, inc=1, device_id=(me, lax.rem(mine + k, groups)), device_id_type=MESH
        )

    arrivals = [
        (f1_ref, filters.at[0]),
        (f2_ref, filters.at[1]),
        (w_ref, w_here),
        (wo_ref, wo_here),
        (x_ref, xg.at[0, mine]),
        (g_ref, xg.at[1, mine]),
    ] + list(zip(sources, tables))
    fetches = []
    for at, (source, target) in enumerate(arrivals):
        fetch = pltpu.make_async_copy(source, target, sems_local.at[at])
        fetch.start()
        fetches.append(fetch)

    def fold(value, first, target, index):
        for q in range(parts):
            target[index + (pl.ds(q * own, own), slice(None))] = value[
                first : first + own, q * LANES : (q + 1) * LANES
            ]

    pl.semaphore_wait(barrier, seqs - 1 + groups - 1)

    def remote(source, target, send_sem, recv_sem, device):
        copy = pltpu.make_async_remote_copy(
            src_ref=source,
            dst_ref=target,
            send_sem=send_sem,
            recv_sem=recv_sem,
            device_id=device,
            device_id_type=MESH,
        )
        copy.start()
        return copy

    x_copies = []
    for a, ref in enumerate((x_ref, g_ref)):
        for k in range(1, groups):
            peer = (me, lax.rem(mine + k, groups))
            x_copies.append(
                remote(ref, xg.at[a, mine], sems_x.at[0, a, k], sems_x.at[1, a, k], peer)
            )

    def exchange(out, into, kind):
        copies = []
        for k in range(1, seqs):
            to = lax.rem(me + k, seqs)
            copies.append(
                remote(
                    out.at[to], into.at[me], sems_seq.at[0, kind, k], sems_seq.at[1, kind, k], (to, mine)
                )
            )
        into[me] = out[me]
        return copies

    def finish(copies):
        for copy in copies:
            copy.wait()

    fetches[0].wait()
    fetches[1].wait()
    for j in range(seqs):
        for i in range(2):
            fold(filters[i, pl.ds(j * own, own), :], 0, filt_out, (j, i))
    filt_copies = exchange(filt_out, filt_in, 0)
    finish(fetches[2:])
    w_turned = w_here[...].reshape(3 * chans, width)
    finish(x_copies[: groups - 1])
    x_all = xg[0].reshape(width, span)
    projected = dot(w_turned, x_all)
    for j in range(seqs):
        for i in range(3):
            fold(projected, i * chans + j * own, sig_fold, (j, i))
    sig_out[...] = sig_fold[:, :3].astype(BF16)
    sig_copies = exchange(sig_out, sig_in, 1)
    finish(x_copies[groups - 1 :])
    g_all = xg[1].reshape(width, span)
    gated_grad_here = dot(wo_here[...], g_all)
    for j in range(seqs):
        fold(gated_grad_here, j * own, sig_fold, (j, 3))
    gg_out[...] = sig_fold[:, 3].astype(BF16)
    sig_copies += exchange(gg_out, gg_in, 8)

    cos_twist = tc_ref[...]
    sin_twist = ts_ref[...]

    def left(table_hi, table_lo, value):
        high, low = split(value)
        return dot(table_hi[...], high) + dot(table_hi[...], low) + dot(table_lo[...], high)

    def right(value, table_hi, table_lo):
        high, low = split(value)
        return dot(high, table_hi[...]) + dot(low, table_hi[...]) + dot(high, table_lo[...])

    def forward(signals):
        joined = signals[0] if len(signals) == 1 else jnp.concatenate(signals, axis=1)
        coarse = left(mf_hi, mf_lo, joined)
        out = []
        for s in range(len(signals)):
            real = coarse[:rows, s * LANES : (s + 1) * LANES]
            imag = coarse[rows:, s * LANES : (s + 1) * LANES]
            turned = jnp.concatenate(
                [
                    real * cos_twist + imag * sin_twist,
                    imag * cos_twist - real * sin_twist,
                ],
                axis=1,
            )
            spectrum = right(turned, df_hi, df_lo)
            out.append((spectrum[:, :LANES], spectrum[:, LANES:]))
        return out

    def inverse(spectra):
        turned = []
        for real, imag in spectra:
            fine = right(jnp.concatenate([real, imag], axis=1), di_hi, di_lo)
            real, imag = fine[:, :LANES], fine[:, LANES:]
            turned.append(
                jnp.concatenate(
                    [
                        real * cos_twist - imag * sin_twist,
                        real * sin_twist + imag * cos_twist,
                    ],
                    axis=0,
                )
            )
        joined = turned[0] if len(turned) == 1 else jnp.concatenate(turned, axis=1)
        result = left(mi_hi, mi_lo, joined)
        return [result[:, s * LANES : (s + 1) * LANES] for s in range(len(spectra))]

    def times(a, b):
        return (a[0] * b[0] - a[1] * b[1], a[0] * b[1] + a[1] * b[0])

    def conj_times(a, b):
        return (a[0] * b[0] + a[1] * b[1], a[0] * b[1] - a[1] * b[0])

    def gathered(block):
        return block.astype(F32).reshape(rows, LANES)

    finish(filt_copies)
    spec_one, spec_two = forward(
        [gathered(filt_in[:, 0]), gathered(filt_in[:, 1])]
    )

    row = lax.broadcasted_iota(jnp.int32, (rows, LANES), 0)
    lane = lax.broadcasted_iota(jnp.int32, (rows, LANES), 1)

    def delayed(value, k):
        rolled = pltpu.roll(value, k, 1)
        before = jnp.where(row < own, 0.0, pltpu.roll(rolled, own, 0))
        return jnp.where(lane < k, before, rolled)

    def advanced(value, k):
        rolled = pltpu.roll(value, LANES - k, 1)
        after = jnp.where(row >= rows - own, 0.0, pltpu.roll(rolled, rows - own, 0))
        return jnp.where(lane >= LANES - k, after, rolled)

    def tap(i, k):
        tile = taps_ref[3 * i + k]
        return jnp.broadcast_to(tile[None], (rows // 8, 8, LANES)).reshape(rows, LANES)

    finish(sig_copies)

    def projection(i):
        value = gathered(sig_in[:, i])
        return value, delayed(value, 1), delayed(value, 2)

    def filtered(i):
        now, one, two = projection(i)
        return tap(i, 0) * now + tap(i, 1) * one + tap(i, 2) * two

    gate_one = filtered(0)
    gate_two = filtered(1)
    value = filtered(2)
    gated_grad = gathered(gg_in[...])

    second_grad = gated_grad * gate_two
    spec_value, spec_second = forward([value, second_grad])
    (first, inner_grad) = inverse([times(spec_one, spec_value), conj_times(spec_two, spec_second)])
    inner = gate_one * first
    gate_one_grad = inner_grad * first
    first_grad = inner_grad * gate_one
    spec_inner, spec_first = forward([inner, first_grad])
    second, filter_two_grad = inverse(
        [times(spec_inner, spec_two), conj_times(spec_inner, spec_second)]
    )
    gated = gate_two * second
    gated_out[...] = gated.reshape(seqs, piece, LANES).astype(BF16)
    gated_copies = exchange(gated_out, gated_in, 2)
    fg_out[1] = (filter_two_grad * scale).reshape(seqs, piece, LANES).astype(BF16)
    fg_copies = exchange(fg_out.at[1], fg_in.at[1], 4)
    value_grad, filter_one_grad = inverse(
        [conj_times(spec_one, spec_first), conj_times(spec_value, spec_first)]
    )
    gate_two_grad = gated_grad * second

    for i, grad in enumerate((gate_one_grad, gate_two_grad, value_grad)):
        back = tap(i, 0) * grad + tap(i, 1) * advanced(grad, 1) + tap(i, 2) * advanced(grad, 2)
        pg_out[:, i] = back.reshape(seqs, piece, LANES).astype(BF16)
    pg_copies = exchange(pg_out, pg_in, 3)
    fg_out[0] = (filter_one_grad * scale).reshape(seqs, piece, LANES).astype(BF16)
    fg_copies += exchange(fg_out.at[0], fg_in.at[0], 7)

    small_lane = lax.broadcasted_iota(jnp.int32, (8, LANES), 1)
    tap_terms = jnp.zeros((8, LANES), F32)
    for i, grad in enumerate((gate_one_grad, gate_two_grad, value_grad)):
        for k, shifted in enumerate(projection(i)):
            total = jnp.sum((grad * shifted).reshape(rows // 8, 8, LANES), axis=0)
            total = jnp.sum(total, axis=1, keepdims=True) * scale
            tap_terms = jnp.where(small_lane == 3 * i + k, total, tap_terms)
    dt_ref[me] = tap_terms
    tap_copies = []
    for k in range(1, seqs):
        to = lax.rem(me + k, seqs)
        tap_copies.append(
            remote(
                dt_ref.at[me], dt_ref.at[me], sems_seq.at[0, 5, k], sems_seq.at[1, 5, k], (to, mine)
            )
        )

    def unfold(value, first, source, target):
        spread(value, first + source * own, own, target)

    finish(gated_copies)
    for j in range(seqs):
        unfold(gated_in[j].astype(F32), 3 * chans, j, grads)
    finish(pg_copies)
    for j in range(seqs):
        for i in range(3):
            unfold(pg_in[j, i].astype(F32), i * chans, j, grads)
    back_all = grads[...].astype(BF16)
    back_in = back_all[: 3 * chans]
    back_out = back_all[3 * chans :]

    dx_part = lax.dot_general(
        w_turned, back_in, (((0,), (0,)), ((), ())), preferred_element_type=F32
    )
    dx_out[...] = dx_part.reshape(groups, chans, span)
    dx_copies = []
    for k in range(1, groups):
        to = lax.rem(mine + k, groups)
        dx_copies.append(
            remote(dx_out.at[to], dx_in.at[mine], sems_dx.at[0, k], sems_dx.at[1, k], (me, to))
        )
    share = width // seqs
    w_out_buf[:, :, : 3 * chans] = (dot_rows(x_all, back_in) * scale).reshape(
        seqs, share, 3 * chans
    ).astype(BF16)
    w_out_buf[:, :, 3 * chans :] = (dot_rows(g_all, back_out) * scale).reshape(seqs, share, chans).astype(BF16)
    w_copies = exchange(w_out_buf, w_in_buf, 6)
    dx_in[mine] = dx_out[mine]

    finish(fg_copies)
    finish(tap_copies)
    finish(dx_copies)
    finish(w_copies)


def closing(w_ref, dt_ref, fg_ref, dx_part_ref, dx_ref, dw_in_ref, taps_ref, df1_ref, df2_ref, dw_out_ref):
    seqs = w_ref.shape[0]
    chans = dx_ref.shape[0]
    own = chans // seqs
    for j in range(seqs):
        for ref, i in ((df1_ref, 0), (df2_ref, 1)):
            spread(fg_ref[i, j].astype(F32), j * own, own, ref)
    total = dx_part_ref[0].astype(F32)
    for j in range(1, dx_part_ref.shape[0]):
        total = total + dx_part_ref[j].astype(F32)
    dx_ref[...] = total.astype(BF16)
    total = w_ref[0].astype(F32)
    for j in range(1, seqs):
        total = total + w_ref[j].astype(F32)
    for i in range(3):
        dw_in_ref[i] = total[:, i * chans : (i + 1) * chans]
    dw_out_ref[...] = total[:, 3 * chans :]
    terms = []
    for j in range(seqs):
        term = dt_ref[j, 0:own]
        for r in range(own, 8, own):
            term = term + dt_ref[j, r : r + own]
        terms.append(term)
    turned = jnp.concatenate(terms, axis=0).T
    for i in range(3):
        taps_ref[i] = turned[3 * i : 3 * i + 3, :]


def local(inputs, cotangent, w_in, short_taps, filter_one, filter_two, w_out):
    chans, span = inputs.shape
    seqs = lax.axis_size("seq")
    groups = lax.axis_size("ch")
    width = chans * groups
    own = chans // seqs
    piece = span // LANES * own
    share = width // seqs
    me = lax.axis_index("seq")
    w_turned = w_in.transpose(0, 2, 1)
    taps = lax.dynamic_slice_in_dim(short_taps.reshape(9, chans), me * own, own, axis=1)
    taps = jnp.broadcast_to(jnp.tile(taps, (1, 8 // own))[:, :, None], (9, 8, LANES))
    tables = [jnp.asarray(table) for table in dft_tables(span * seqs, own)]
    vmem = pl.BlockSpec(memory_space=pltpu.VMEM)
    hbm = pl.BlockSpec(memory_space=pltpu.HBM)
    received = pl.pallas_call(
        functools.partial(kernel, seqs, groups),
        out_shape=(
            jax.ShapeDtypeStruct((seqs, share, 4 * chans), BF16),
            jax.ShapeDtypeStruct((seqs, 8, LANES), F32),
            jax.ShapeDtypeStruct((2, seqs, piece, LANES), BF16),
            jax.ShapeDtypeStruct((groups, chans, span), F32),
        ),
        in_specs=[hbm] * 6 + [vmem] + [hbm] * TABLES,
        out_specs=(vmem,) * 4,
        scratch_shapes=[pltpu.VMEM(table.shape, table.dtype) for table in tables]
        + [
            pltpu.VMEM((2, chans, span), F32),
            pltpu.VMEM(w_turned.shape, BF16),
            pltpu.VMEM(w_out.shape, BF16),
            pltpu.VMEM((2, groups, chans, span), BF16),
            pltpu.VMEM((seqs, 2, piece, LANES), F32),
            pltpu.VMEM((seqs, 2, piece, LANES), F32),
            pltpu.VMEM((seqs, 4, piece, LANES), F32),
            pltpu.VMEM((seqs, 3, piece, LANES), BF16),
            pltpu.VMEM((seqs, 3, piece, LANES), BF16),
            pltpu.VMEM((seqs, piece, LANES), BF16),
            pltpu.VMEM((seqs, piece, LANES), BF16),
            pltpu.VMEM((seqs, piece, LANES), BF16),
            pltpu.VMEM((seqs, piece, LANES), BF16),
            pltpu.VMEM((2, seqs, piece, LANES), BF16),
            pltpu.VMEM((seqs, 3, piece, LANES), BF16),
            pltpu.VMEM((seqs, 3, piece, LANES), BF16),
            pltpu.VMEM((4 * chans, span), F32),
            pltpu.VMEM((seqs, share, 4 * chans), BF16),
            pltpu.VMEM((groups, chans, span), F32),
            pltpu.SemaphoreType.DMA((2, 2, groups)),
            pltpu.SemaphoreType.DMA((2, 9, seqs)),
            pltpu.SemaphoreType.DMA((2, groups)),
            pltpu.SemaphoreType.DMA((6 + TABLES,)),
        ],
        compiler_params=pltpu.CompilerParams(
            collective_id=0, has_side_effects=True, vmem_limit_bytes=60 * 1024 * 1024
        ),
    )(inputs, cotangent, filter_one, filter_two, w_turned, w_out, taps, *tables)
    dx, w_in_grad, taps_grad, df1, df2, w_out_turned = (
        pl.pallas_call(
            closing,
            out_shape=(
                jax.ShapeDtypeStruct((chans, span), BF16),
                jax.ShapeDtypeStruct((3, share, chans), F32),
                jax.ShapeDtypeStruct((3, 3, chans), F32),
                jax.ShapeDtypeStruct((chans, span), F32),
                jax.ShapeDtypeStruct((chans, span), F32),
                jax.ShapeDtypeStruct((share, chans), F32),
            ),
            in_specs=[vmem] * 4,
            out_specs=(vmem,) * 6,
            compiler_params=pltpu.CompilerParams(vmem_limit_bytes=60 * 1024 * 1024),
        )(*received)
    )
    return (dx, w_in_grad, taps_grad, df1, df2, w_out_turned.T)


def solution(mesh):
    in_specs = (
        P("ch", "seq"),
        P("ch", "seq"),
        P(None, None, "ch"),
        P(None, None, "ch"),
        P("ch", "seq"),
        P("ch", "seq"),
        P("ch", None),
    )
    out_specs = (
        P("ch", "seq"),
        P(None, "seq", "ch"),
        P(None, None, "ch"),
        P("ch", "seq"),
        P("ch", "seq"),
        P("ch", "seq"),
    )
    return jax.shard_map(local, mesh=mesh, in_specs=in_specs, out_specs=out_specs, check_vma=False)
```

```python
import functools
import math

import jax
import jax.numpy as jnp
import ml_dtypes
import numpy as np
from jax import lax
from jax.experimental import pallas as pl
from jax.experimental.pallas import tpu as pltpu
from jax.sharding import PartitionSpec as P

LANES = 128
TABLES = 10
MESH = pl.DeviceIdType.MESH
BF16 = jnp.bfloat16
F32 = jnp.float32


def halves(table):
    high = table.astype(np.float32).astype(ml_dtypes.bfloat16)
    low = (table - high.astype(np.float64)).astype(np.float32).astype(ml_dtypes.bfloat16)
    return [high, low]


def dft_tables(tokens, chans):
    blocks = tokens // LANES
    size = 2 * tokens
    eye = np.eye(chans)
    place = np.arange(blocks, dtype=np.float64)
    half = np.arange(blocks, dtype=np.float64) + 0.5
    coarse = 2.0 * np.pi / (2 * blocks) * np.outer(half, place)
    cos_one, sin_one = np.cos(coarse), np.sin(coarse)
    forward_one = np.concatenate([np.kron(cos_one, eye), -np.kron(sin_one, eye)], axis=0)
    inverse_one = 2.0 / size * np.concatenate(
        [np.kron(cos_one.T, eye), -np.kron(sin_one.T, eye)], axis=1
    )
    lane = np.arange(LANES)
    fine = 2.0 * np.pi / LANES * (np.outer(lane, lane) % LANES)
    cos_two, sin_two = np.cos(fine), np.sin(fine)
    forward_two = np.block([[cos_two, -sin_two], [sin_two, cos_two]])
    inverse_two = np.block([[cos_two, sin_two], [-sin_two, cos_two]])
    twist = np.repeat(2.0 * np.pi / size * np.outer(half, lane), chans, axis=0)
    tables = halves(forward_one) + halves(inverse_one) + halves(forward_two) + halves(inverse_two)
    return tables + [np.cos(twist).astype(np.float32), np.sin(twist).astype(np.float32)]


def split(value):
    high = value.astype(BF16)
    return high, (value - high.astype(F32)).astype(BF16)


def dot(left, right):
    return jnp.dot(left, right, preferred_element_type=F32)


def dot_rows(left, right):
    return lax.dot_general(left, right, (((1,), (1,)), ((), ())), preferred_element_type=F32)


def spread(value, first, own, target):
    for q in range(target.shape[1] // LANES):
        target[first : first + own, q * LANES : (q + 1) * LANES] = value[q * own : (q + 1) * own]


def kernel(
    seqs,
    groups,
    x_ref,
    g_ref,
    f1_ref,
    f2_ref,
    w_ref,
    wo_ref,
    taps_ref,
    *rest,
):
    sources, rest = rest[:TABLES], rest[TABLES:]
    w_in_buf, dt_ref, fg_in, dx_in = rest[:4]
    tables, rest = rest[4 : 4 + TABLES], rest[4 + TABLES :]
    mf_hi, mf_lo, mi_hi, mi_lo, df_hi, df_lo, di_hi, di_lo, tc_ref, ts_ref = tables
    (
        filters,
        w_here,
        wo_here,
        xg,
        filt_out,
        filt_in,
        sig_fold,
        sig_out,
        sig_in,
        gg_out,
        gg_in,
        gated_out,
        gated_in,
        fg_out,
        pg_out,
        pg_in,
        grads,
        w_out_buf,
        dx_out,
        sems_x,
        sems_seq,
        sems_dx,
        sems_local,
    ) = rest
    chans, span = x_ref.shape
    own = chans // seqs
    parts = span // LANES
    piece = parts * own
    rows = piece * seqs
    width = chans * groups
    scale = 1.0 / math.sqrt(span * seqs)
    me = lax.axis_index("seq")
    mine = lax.axis_index("ch")

    barrier = pltpu.get_barrier_semaphore()
    for k in range(1, seqs):
        pl.semaphore_signal(
            barrier, inc=1, device_id=(lax.rem(me + k, seqs), mine), device_id_type=MESH
        )
    for k in range(1, groups):
        pl.semaphore_signal(
            barrier, inc=1, device_id=(me, lax.rem(mine + k, groups)), device_id_type=MESH
        )

    arrivals = [
        (f1_ref, filters.at[0]),
        (f2_ref, filters.at[1]),
        (w_ref, w_here),
        (wo_ref, wo_here),
        (x_ref, xg.at[0, mine]),
        (g_ref, xg.at[1, mine]),
    ] + list(zip(sources, tables))
    fetches = []
    for at, (source, target) in enumerate(arrivals):
        fetch = pltpu.make_async_copy(source, target, sems_local.at[at])
        fetch.start()
        fetches.append(fetch)

    def fold(value, first, target, index):
        for q in range(parts):
            target[index + (pl.ds(q * own, own), slice(None))] = value[
                first : first + own, q * LANES : (q + 1) * LANES
            ]

    pl.semaphore_wait(barrier, seqs - 1 + groups - 1)

    def remote(source, target, send_sem, recv_sem, device):
        copy = pltpu.make_async_remote_copy(
            src_ref=source,
            dst_ref=target,
            send_sem=send_sem,
            recv_sem=recv_sem,
            device_id=device,
            device_id_type=MESH,
        )
        copy.start()
        return copy

    x_copies = []
    for a, ref in enumerate((x_ref, g_ref)):
        for k in range(1, groups):
            peer = (me, lax.rem(mine + k, groups))
            x_copies.append(
                remote(ref, xg.at[a, mine], sems_x.at[0, a, k], sems_x.at[1, a, k], peer)
            )

    def exchange(out, into, kind):
        copies = []
        for k in range(1, seqs):
            to = lax.rem(me + k, seqs)
            copies.append(
                remote(
                    out.at[to], into.at[me], sems_seq.at[0, kind, k], sems_seq.at[1, kind, k], (to, mine)
                )
            )
        into[me] = out[me]
        return copies

    def finish(copies):
        for copy in copies:
            copy.wait()

    fetches[0].wait()
    fetches[1].wait()
    for j in range(seqs):
        for i in range(2):
            fold(filters[i, pl.ds(j * own, own), :], 0, filt_out, (j, i))
    filt_copies = exchange(filt_out, filt_in, 0)
    finish(fetches[2:])
    w_turned = w_here[...].reshape(3 * chans, width)
    finish(x_copies[: groups - 1])
    x_all = xg[0].reshape(width, span)
    projected = dot(w_turned, x_all)
    for j in range(seqs):
        for i in range(3):
            fold(projected, i * chans + j * own, sig_fold, (j, i))
    sig_out[...] = sig_fold[:, :3].astype(BF16)
    sig_copies = exchange(sig_out, sig_in, 1)
    finish(x_copies[groups - 1 :])
    g_all = xg[1].reshape(width, span)
    gated_grad_here = dot(wo_here[...], g_all)
    for j in range(seqs):
        fold(gated_grad_here, j * own, sig_fold, (j, 3))
    gg_out[...] = sig_fold[:, 3].astype(BF16)
    sig_copies += exchange(gg_out, gg_in, 8)

    cos_twist = tc_ref[...]
    sin_twist = ts_ref[...]

    def left(table_hi, table_lo, value):
        high, low = split(value)
        return dot(table_hi[...], high) + dot(table_hi[...], low) + dot(table_lo[...], high)

    def right(value, table_hi, table_lo):
        high, low = split(value)
        return dot(high, table_hi[...]) + dot(low, table_hi[...]) + dot(high, table_lo[...])

    def forward(signals):
        joined = signals[0] if len(signals) == 1 else jnp.concatenate(signals, axis=1)
        coarse = left(mf_hi, mf_lo, joined)
        out = []
        for s in range(len(signals)):
            real = coarse[:rows, s * LANES : (s + 1) * LANES]
            imag = coarse[rows:, s * LANES : (s + 1) * LANES]
            turned = jnp.concatenate(
                [
                    real * cos_twist + imag * sin_twist,
                    imag * cos_twist - real * sin_twist,
                ],
                axis=1,
            )
            spectrum = right(turned, df_hi, df_lo)
            out.append((spectrum[:, :LANES], spectrum[:, LANES:]))
        return out

    def inverse(spectra):
        turned = []
        for real, imag in spectra:
            fine = right(jnp.concatenate([real, imag], axis=1), di_hi, di_lo)
            real, imag = fine[:, :LANES], fine[:, LANES:]
            turned.append(
                jnp.concatenate(
                    [
                        real * cos_twist - imag * sin_twist,
                        real * sin_twist + imag * cos_twist,
                    ],
                    axis=0,
                )
            )
        joined = turned[0] if len(turned) == 1 else jnp.concatenate(turned, axis=1)
        result = left(mi_hi, mi_lo, joined)
        return [result[:, s * LANES : (s + 1) * LANES] for s in range(len(spectra))]

    def times(a, b):
        return (a[0] * b[0] - a[1] * b[1], a[0] * b[1] + a[1] * b[0])

    def conj_times(a, b):
        return (a[0] * b[0] + a[1] * b[1], a[0] * b[1] - a[1] * b[0])

    def gathered(block):
        return block.astype(F32).reshape(rows, LANES)

    finish(filt_copies)
    spec_one, spec_two = forward(
        [gathered(filt_in[:, 0]), gathered(filt_in[:, 1])]
    )

    row = lax.broadcasted_iota(jnp.int32, (rows, LANES), 0)
    lane = lax.broadcasted_iota(jnp.int32, (rows, LANES), 1)

    def delayed(value, k):
        rolled = pltpu.roll(value, k, 1)
        before = jnp.where(row < own, 0.0, pltpu.roll(rolled, own, 0))
        return jnp.where(lane < k, before, rolled)

    def advanced(value, k):
        rolled = pltpu.roll(value, LANES - k, 1)
        after = jnp.where(row >= rows - own, 0.0, pltpu.roll(rolled, rows - own, 0))
        return jnp.where(lane >= LANES - k, after, rolled)

    def tap(i, k):
        at = 3 * i + k
        tile = jnp.broadcast_to(taps_ref[:, at : at + 1], (8, LANES))
        return jnp.broadcast_to(tile[None], (rows // 8, 8, LANES)).reshape(rows, LANES)

    finish(sig_copies)

    def projection(i):
        value = gathered(sig_in[:, i])
        return value, delayed(value, 1), delayed(value, 2)

    def filtered(i):
        now, one, two = projection(i)
        return tap(i, 0) * now + tap(i, 1) * one + tap(i, 2) * two

    gate_one = filtered(0)
    gate_two = filtered(1)
    value = filtered(2)
    gated_grad = gathered(gg_in[...])

    second_grad = gated_grad * gate_two
    spec_value, spec_second = forward([value, second_grad])
    (first, inner_grad) = inverse([times(spec_one, spec_value), conj_times(spec_two, spec_second)])
    inner = gate_one * first
    gate_one_grad = inner_grad * first
    first_grad = inner_grad * gate_one
    spec_inner, spec_first = forward([inner, first_grad])
    second, filter_two_grad = inverse(
        [times(spec_inner, spec_two), conj_times(spec_inner, spec_second)]
    )
    gated = gate_two * second
    gated_out[...] = gated.reshape(seqs, piece, LANES).astype(BF16)
    gated_copies = exchange(gated_out, gated_in, 2)
    fg_out[1] = (filter_two_grad * scale).reshape(seqs, piece, LANES).astype(BF16)
    fg_copies = exchange(fg_out.at[1], fg_in.at[1], 4)
    value_grad, filter_one_grad = inverse(
        [conj_times(spec_one, spec_first), conj_times(spec_value, spec_first)]
    )
    gate_two_grad = gated_grad * second

    for i, grad in enumerate((gate_one_grad, gate_two_grad, value_grad)):
        back = tap(i, 0) * grad + tap(i, 1) * advanced(grad, 1) + tap(i, 2) * advanced(grad, 2)
        pg_out[:, i] = back.reshape(seqs, piece, LANES).astype(BF16)
    pg_copies = exchange(pg_out, pg_in, 3)
    fg_out[0] = (filter_one_grad * scale).reshape(seqs, piece, LANES).astype(BF16)
    fg_copies += exchange(fg_out.at[0], fg_in.at[0], 7)

    small_lane = lax.broadcasted_iota(jnp.int32, (8, LANES), 1)
    tap_terms = jnp.zeros((8, LANES), F32)
    for i, grad in enumerate((gate_one_grad, gate_two_grad, value_grad)):
        for k, shifted in enumerate(projection(i)):
            total = jnp.sum((grad * shifted).reshape(rows // 8, 8, LANES), axis=0)
            total = jnp.sum(total, axis=1, keepdims=True) * scale
            tap_terms = jnp.where(small_lane == 3 * i + k, total, tap_terms)
    dt_ref[me] = tap_terms
    tap_copies = []
    for k in range(1, seqs):
        to = lax.rem(me + k, seqs)
        tap_copies.append(
            remote(
                dt_ref.at[me], dt_ref.at[me], sems_seq.at[0, 5, k], sems_seq.at[1, 5, k], (to, mine)
            )
        )

    def unfold(value, first, source, target):
        spread(value, first + source * own, own, target)

    finish(gated_copies)
    for j in range(seqs):
        unfold(gated_in[j].astype(F32), 3 * chans, j, grads)
    share = width // seqs
    back_out = grads[pl.ds(3 * chans, chans), :].astype(BF16)
    w_out_buf[:, :, 3 * chans :] = (
        (dot_rows(g_all, back_out) * scale).reshape(seqs, share, chans).astype(BF16)
    )
    finish(pg_copies)
    for j in range(seqs):
        for i in range(3):
            unfold(pg_in[j, i].astype(F32), i * chans, j, grads)
    back_in = grads[pl.ds(0, 3 * chans), :].astype(BF16)

    dx_part = lax.dot_general(
        w_turned, back_in, (((0,), (0,)), ((), ())), preferred_element_type=F32
    )
    dx_out[...] = dx_part.reshape(groups, chans, span)
    dx_copies = []
    for k in range(1, groups):
        to = lax.rem(mine + k, groups)
        dx_copies.append(
            remote(dx_out.at[to], dx_in.at[mine], sems_dx.at[0, k], sems_dx.at[1, k], (me, to))
        )
    w_out_buf[:, :, : 3 * chans] = (dot_rows(x_all, back_in) * scale).reshape(
        seqs, share, 3 * chans
    ).astype(BF16)
    w_copies = exchange(w_out_buf, w_in_buf, 6)
    dx_in[mine] = dx_out[mine]

    finish(fg_copies)
    finish(tap_copies)
    finish(dx_copies)
    finish(w_copies)


def closing(w_ref, dt_ref, fg_ref, dx_part_ref, dx_ref, dw_in_ref, taps_ref, df1_ref, df2_ref, dw_out_ref):
    seqs = w_ref.shape[0]
    chans = dx_ref.shape[0]
    own = chans // seqs
    for j in range(seqs):
        for ref, i in ((df1_ref, 0), (df2_ref, 1)):
            spread(fg_ref[i, j].astype(F32), j * own, own, ref)
    total = dx_part_ref[0].astype(F32)
    for j in range(1, dx_part_ref.shape[0]):
        total = total + dx_part_ref[j].astype(F32)
    dx_ref[...] = total.astype(BF16)
    total = w_ref[0].astype(F32)
    for j in range(1, seqs):
        total = total + w_ref[j].astype(F32)
    for i in range(3):
        dw_in_ref[i] = total[:, i * chans : (i + 1) * chans]
    dw_out_ref[...] = total[:, 3 * chans :]
    terms = []
    for j in range(seqs):
        term = dt_ref[j, 0:own]
        for r in range(own, 8, own):
            term = term + dt_ref[j, r : r + own]
        terms.append(term)
    turned = jnp.concatenate(terms, axis=0).T
    for i in range(3):
        taps_ref[i] = turned[3 * i : 3 * i + 3, :]


def local(inputs, cotangent, w_in, short_taps, filter_one, filter_two, w_out):
    chans, span = inputs.shape
    seqs = lax.axis_size("seq")
    groups = lax.axis_size("ch")
    width = chans * groups
    own = chans // seqs
    piece = span // LANES * own
    share = width // seqs
    me = lax.axis_index("seq")
    w_turned = w_in.transpose(0, 2, 1)
    taps = lax.dynamic_slice_in_dim(short_taps.reshape(9, chans), me * own, own, axis=1)
    taps = jnp.tile(taps, (1, 8 // own)).T
    tables = [jnp.asarray(table) for table in dft_tables(span * seqs, own)]
    vmem = pl.BlockSpec(memory_space=pltpu.VMEM)
    hbm = pl.BlockSpec(memory_space=pltpu.HBM)
    received = pl.pallas_call(
        functools.partial(kernel, seqs, groups),
        out_shape=(
            jax.ShapeDtypeStruct((seqs, share, 4 * chans), BF16),
            jax.ShapeDtypeStruct((seqs, 8, LANES), F32),
            jax.ShapeDtypeStruct((2, seqs, piece, LANES), BF16),
            jax.ShapeDtypeStruct((groups, chans, span), F32),
        ),
        in_specs=[hbm] * 6 + [vmem] + [hbm] * TABLES,
        out_specs=(vmem,) * 4,
        scratch_shapes=[pltpu.VMEM(table.shape, table.dtype) for table in tables]
        + [
            pltpu.VMEM((2, chans, span), F32),
            pltpu.VMEM(w_turned.shape, BF16),
            pltpu.VMEM(w_out.shape, BF16),
            pltpu.VMEM((2, groups, chans, span), BF16),
            pltpu.VMEM((seqs, 2, piece, LANES), F32),
            pltpu.VMEM((seqs, 2, piece, LANES), F32),
            pltpu.VMEM((seqs, 4, piece, LANES), F32),
            pltpu.VMEM((seqs, 3, piece, LANES), BF16),
            pltpu.VMEM((seqs, 3, piece, LANES), BF16),
            pltpu.VMEM((seqs, piece, LANES), BF16),
            pltpu.VMEM((seqs, piece, LANES), BF16),
            pltpu.VMEM((seqs, piece, LANES), BF16),
            pltpu.VMEM((seqs, piece, LANES), BF16),
            pltpu.VMEM((2, seqs, piece, LANES), BF16),
            pltpu.VMEM((seqs, 3, piece, LANES), BF16),
            pltpu.VMEM((seqs, 3, piece, LANES), BF16),
            pltpu.VMEM((4 * chans, span), F32),
            pltpu.VMEM((seqs, share, 4 * chans), BF16),
            pltpu.VMEM((groups, chans, span), F32),
            pltpu.SemaphoreType.DMA((2, 2, groups)),
            pltpu.SemaphoreType.DMA((2, 9, seqs)),
            pltpu.SemaphoreType.DMA((2, groups)),
            pltpu.SemaphoreType.DMA((6 + TABLES,)),
        ],
        compiler_params=pltpu.CompilerParams(
            collective_id=0, has_side_effects=True, vmem_limit_bytes=60 * 1024 * 1024
        ),
    )(inputs, cotangent, filter_one, filter_two, w_turned, w_out, taps, *tables)
    dx, w_in_grad, taps_grad, df1, df2, w_out_turned = (
        pl.pallas_call(
            closing,
            out_shape=(
                jax.ShapeDtypeStruct((chans, span), BF16),
                jax.ShapeDtypeStruct((3, share, chans), F32),
                jax.ShapeDtypeStruct((3, 3, chans), F32),
                jax.ShapeDtypeStruct((chans, span), F32),
                jax.ShapeDtypeStruct((chans, span), F32),
                jax.ShapeDtypeStruct((share, chans), F32),
            ),
            in_specs=[vmem] * 4,
            out_specs=(vmem,) * 6,
            compiler_params=pltpu.CompilerParams(vmem_limit_bytes=60 * 1024 * 1024),
        )(*received)
    )
    return (dx, w_in_grad, taps_grad, df1, df2, w_out_turned.T)


def solution(mesh):
    in_specs = (
        P("ch", "seq"),
        P("ch", "seq"),
        P(None, None, "ch"),
        P(None, None, "ch"),
        P("ch", "seq"),
        P("ch", "seq"),
        P("ch", None),
    )
    out_specs = (
        P("ch", "seq"),
        P(None, "seq", "ch"),
        P(None, None, "ch"),
        P("ch", "seq"),
        P("ch", "seq"),
        P("ch", "seq"),
    )
    return jax.shard_map(local, mesh=mesh, in_specs=in_specs, out_specs=out_specs, check_vma=False)
```
